32 devices in a mesh: groups: 2 (over y), energy: 4 (over z), tile: 2 (over x), mode: 2 (over core).
Axes of the slice: x: 2, y: 2, z: 4, core: 2. Of those that a mesh axis runs over, the one named last changes fastest.
Arguments:
- object_field: float32 [2, 16, 256, 192], P(None, ('groups', 'energy', 'mode'), 'tile'), parts along dimension 1, may hold values from -6 to 6
- probe_field: float32 [2, 3, 16, 128, 128], P(None, None, ('groups', 'energy', 'mode')), parts along dimension 2, may hold values from -6 to 6
- modulus: bfloat16 [16, 16, 128, 128], P(('groups', 'energy', 'mode'), 'tile'), parts along dimension 0, may hold values from 0 to 2
- offsets: int32 [32, 2], P(('groups', 'tile')), parts along dimension 0, may hold values from 0 to 31
- spectra_basis: float32 [8, 8], replicated, may hold values from -2 to 2
- analysis: float32 [8, 8], replicated, may hold values from -2 to 2
- threshold: float32 [8], replicated, may hold values from 0.05 to 0.5
Outputs:
- object_out: float32 [2, 16, 256, 192], P(None, ('groups', 'energy', 'mode'), 'tile'), parts along dimension 1
- probe_out: float32 [2, 3, 16, 128, 128], P(None, None, ('groups', 'energy', 'mode')), parts along dimension 2
The draws below stay inside these ranges and needn't reach their ends.
There are 2 independent parts, one for each index of `groups`. The reference program is written for one: setup_inputs(seed, part) draws one part's arguments, and reference() takes and returns one part's arrays. A program takes and returns all parts, laid end to end along the dimension named above; an argument that names none is the same for every part. Nothing has to cross between parts.
All inputs are finite; a program needn't handle non-finite values.
Results may differ from the reference program's by a relative error of at most 0.0033.
Values may be sent and summed in bfloat16 or wider, within the bound.
A program may use at most 128 MiB of HBM per device.

```python
import math
import jax
import jax.numpy as jnp
from jax import lax

PSIZE = 128
MODES = 3
COMPS = 8
ITERS = 1
PCOLS = 2
STEP = 32
TILE_ROWS = 128
WIDTH_COLS = 192
ROWS_ALL = 256
POS_DEV = 8
POS = 16
ENERGIES = 8


def touch_ends(result, key, smallest, high):
    place = [jax.random.randint(jax.random.fold_in(key, axis), (), 0, length) for axis, length in enumerate(result.shape)]
    longest = result.shape.index(max(result.shape))
    neighbour = place[:longest] + [(place[longest] + 1) % result.shape[longest]] + place[longest + 1:]
    return result.at[tuple(place)].set(smallest).at[tuple(neighbour)].set(high)


def block_scale(rng, dims, split, smallest, largest):
    def one(dim, blocks):
        heights = jax.random.uniform(jax.random.fold_in(jax.random.fold_in(rng, 6), dim), (blocks,), jnp.float32, smallest / len(split), largest / len(split))
        return jnp.repeat(jnp.exp(heights), dims[dim] // blocks).reshape((-1,) + (1,) * (len(dims) - dim - 1))

    gain = one(*split[0])
    for cut in split[1:]:
        gain = gain * one(*cut)
    return gain


def scatter_about(own_key, dims, deviation, limit, shards=(), held_as=jnp.bfloat16):
    values = jax.random.normal(own_key, dims, jnp.float32) * deviation
    if len(shards) > 0:
        values = block_scale(own_key, dims, shards, -0.22, 0.18) * values
    return jnp.clip(values, min=-limit, max=limit).astype(held_as)


def setup_inputs(seed: int = 0, part: int = 0) -> dict:
    splits = jax.random.split(jax.random.key(seed), 8)
    part_keys = jax.random.split(jax.random.fold_in(splits[7], part), 8)
    object_field = scatter_about(part_keys[0], (2, ENERGIES, ROWS_ALL, WIDTH_COLS), 1.0, 6.0, ((1, 8), (2, 2)), jnp.float32)
    probe_field = scatter_about(part_keys[1], (2, MODES, ENERGIES, PSIZE, PSIZE), 0.6, 6.0, ((2, 8),), jnp.float32)
    modulus = jnp.clip(2.0 * jax.random.uniform(part_keys[2], (ENERGIES, POS, PSIZE, PSIZE), jnp.float32) ** block_scale(part_keys[2], (ENERGIES, POS, PSIZE, PSIZE), ((0, 8), (1, 2)), -0.2, 0.2), 0.0, 2.0).astype(jnp.bfloat16)
    offsets = touch_ends(jax.random.randint(part_keys[3], (POS, 2), 0, STEP), jax.random.fold_in(part_keys[3], 1), 0, STEP - 1).astype(jnp.int32)
    spectra_basis = scatter_about(splits[4], (ENERGIES, COMPS), COMPS ** -0.5, 2.0, (), jnp.float32)
    analysis = scatter_about(splits[5], (COMPS, ENERGIES), ENERGIES ** -0.5, 2.0, (), jnp.float32)
    threshold = jnp.clip(jnp.exp(jax.random.uniform(splits[6], (COMPS,), jnp.float32, math.log(0.05), math.log(0.5))), 0.05, 0.5)
    return {"object_field": object_field, "probe_field": probe_field, "modulus": modulus, "offsets": offsets, "spectra_basis": spectra_basis, "analysis": analysis, "threshold": threshold}


per_block = 8

def dft_tables(extent):
    counter = jnp.arange(extent, dtype=jnp.int32)
    products_mod = counter[:, None] * counter[None, :] % extent
    phases = -2.0 * math.pi / extent * products_mod.astype(jnp.float32)
    normalizer = 1.0 / math.sqrt(extent)
    cosine = jnp.cos(phases) * normalizer
    sine_table = jnp.sin(phases) * normalizer
    forward = jnp.concatenate([jnp.concatenate([cosine, -sine_table], axis=1), jnp.concatenate([sine_table, cosine], axis=1)], axis=0).astype(jnp.bfloat16)
    backward = jnp.concatenate([jnp.concatenate([cosine, sine_table], axis=1), jnp.concatenate([-sine_table, cosine], axis=1)], axis=0).astype(jnp.bfloat16)
    return (forward, backward)

def product(form, left_op, right_op):
    return jnp.einsum(form, left_op.astype(jnp.float32), right_op.astype(jnp.float32))

def wave_block(extended, probe_now, block_moduli, row_starts, col_starts, tables, multiply):
    extent = probe_now.shape[-1]
    members = block_moduli.shape[0]
    modes_here = probe_now.shape[1]
    anchor = jnp.zeros((), jnp.int32)

    def cut_patch(row_start, col_start):
        return lax.dynamic_slice(extended, (anchor, row_start, col_start), (2, extent, extent))
    patches = jax.vmap(cut_patch)(row_starts, col_starts)
    object_real = patches[:, 0:1]
    object_imag = patches[:, 1:2]
    probe_real = probe_now[0][None]
    probe_imag = probe_now[1][None]
    wave_real = probe_real * object_real - probe_imag * object_imag
    wave_imag = probe_real * object_imag + probe_imag * object_real
    stacked = jnp.concatenate([wave_real, wave_imag], axis=2)
    forward, backward = tables
    batch = stacked.reshape(members * modes_here, 2 * extent, extent).astype(jnp.bfloat16)
    halfway = multiply('ij,bjk->bik', forward, batch)
    columns = jnp.concatenate([halfway[:, :extent], halfway[:, extent:]], axis=2).astype(jnp.bfloat16)
    spectrum = multiply('bik,kl->bil', columns, backward).reshape(members, modes_here, extent, 2 * extent)
    squares = lax.optimization_barrier(jnp.sum(spectrum * spectrum, axis=1))
    magnitude_sq = squares[:, :, :extent] + squares[:, :, extent:]
    factor = block_moduli.astype(spectrum.dtype) / jnp.sqrt(magnitude_sq + 0.01)
    scaled = (spectrum * jnp.concatenate([factor, factor], axis=2)[:, None]).astype(jnp.bfloat16)
    scaled = scaled.reshape(members * modes_here, extent, 2 * extent)
    returned = multiply('bik,kl->bil', scaled, forward)
    restacked = jnp.concatenate([returned[:, :, :extent], returned[:, :, extent:]], axis=1).astype(jnp.bfloat16)
    new_wave = multiply('ij,bjk->bik', backward, restacked).reshape(members, modes_here, 2 * extent, extent)
    change = new_wave - stacked
    change_real = change[:, :, :extent]
    change_imag = change[:, :, extent:]
    numerator = jnp.stack([lax.optimization_barrier(jnp.sum(probe_real * change_real + probe_imag * change_imag, axis=1)), lax.optimization_barrier(jnp.sum(probe_real * change_imag - probe_imag * change_real, axis=1))], axis=1)
    probe_num = jnp.stack([lax.optimization_barrier(jnp.sum(object_real * change_real + object_imag * change_imag, axis=0)), lax.optimization_barrier(jnp.sum(object_real * change_imag - object_imag * change_real, axis=0))], axis=0)
    probe_den = lax.optimization_barrier(jnp.sum(object_real * object_real + object_imag * object_imag, axis=(0, 1)))
    return (numerator, probe_num, probe_den)

def accumulate(extended, probe_now, probe_power, moduli, row_starts, col_starts, tables, multiply):
    extent = probe_now.shape[-1]
    blocks = moduli.shape[0] // per_block
    anchor = jnp.zeros((), jnp.int32)

    def one_block(running, operands):
        sum_wave, sum_weight, probe_num, probe_den = running
        block_moduli, block_rows, block_cols = operands
        numerator, block_num, block_den = wave_block(extended, probe_now, block_moduli, block_rows, block_cols, tables, multiply)
        for member in range(per_block):
            corner = (anchor, block_rows[member], block_cols[member])
            sum_wave = lax.dynamic_update_slice(sum_wave, lax.dynamic_slice(sum_wave, corner, (2, extent, extent)) + numerator[member], corner)
            flat_corner = (block_rows[member], block_cols[member])
            sum_weight = lax.dynamic_update_slice(sum_weight, lax.dynamic_slice(sum_weight, flat_corner, (extent, extent)) + probe_power, flat_corner)
        return ((sum_wave, sum_weight, probe_num + block_num, probe_den + block_den), None)
    start_state = (jnp.zeros_like(extended), jnp.zeros(extended.shape[1:], extended.dtype), jnp.zeros_like(probe_now), jnp.zeros((extent, extent), probe_now.dtype))
    operands = (moduli.reshape(blocks, per_block, extent, extent), row_starts.reshape(blocks, per_block), col_starts.reshape(blocks, per_block))
    final_state, unused = lax.scan(one_block, start_state, operands)
    return final_state

def spectral(spectra, spectra_basis, analysis, threshold):
    coefficient = jnp.einsum('ke,xep->xkp', analysis, spectra, precision=lax.Precision.HIGHEST)
    shrunk = jnp.sign(coefficient) * jnp.maximum(jnp.abs(coefficient) - threshold[None, :, None], 0.0)
    projected = jnp.einsum('ek,xkp->xep', spectra_basis, shrunk, precision=lax.Precision.HIGHEST)
    return 0.5 * spectra + 0.5 * projected

def reference(object_field, probe_field, modulus, offsets, spectra_basis, analysis, threshold):
    extent = PSIZE
    tables = dft_tables(extent)
    counter = jnp.arange(POS, dtype=jnp.int32)
    within = counter % POS_DEV
    owner_tile = counter // POS_DEV
    row_starts = (owner_tile * TILE_ROWS + STEP * (within // PCOLS) + offsets[:, 0]).astype(jnp.int32)
    col_starts = (STEP * (within % PCOLS) + offsets[:, 1]).astype(jnp.int32)
    object_now = jnp.transpose(object_field, (1, 0, 2, 3))
    probe_now = jnp.transpose(probe_field, (2, 0, 1, 3, 4))
    for sweep in range(ITERS):

        def one_energy(operands):
            object_e, probe_e, moduli_e = operands
            rounded = lax.optimization_barrier(object_e.astype(jnp.bfloat16)).astype(object_e.dtype)
            extended = jnp.pad(rounded, ((0, 0), (0, extent), (0, 0)))
            probe_power = lax.optimization_barrier(jnp.sum(probe_e * probe_e, axis=(0, 1)))
            sum_wave, sum_weight, probe_num, probe_den = accumulate(extended, probe_e, probe_power, moduli_e, row_starts, col_starts, tables, product)
            object_new = object_e + sum_wave[:, :ROWS_ALL] / (sum_weight[:ROWS_ALL] + 0.1 * jnp.max(probe_power) + 1e-06)
            probe_new = probe_e + probe_num / (probe_den + 0.1 * jnp.max(probe_den) + 1e-06)
            return (object_new, probe_new)
        object_now, probe_now = lax.map(one_energy, (object_now, probe_now, modulus))
        spectra = jnp.transpose(object_now, (1, 0, 2, 3)).reshape(2, ENERGIES, ROWS_ALL * WIDTH_COLS)
        spectra = spectral(spectra, spectra_basis, analysis, threshold)
        object_now = jnp.transpose(spectra.reshape(2, ENERGIES, ROWS_ALL, WIDTH_COLS), (1, 0, 2, 3))
    return (jnp.transpose(object_now, (1, 0, 2, 3)), jnp.transpose(probe_now, (1, 2, 0, 3, 4)))
```

```python
import functools
import math

import jax
import jax.numpy as jnp
import numpy as np
from jax import lax
from jax.experimental import pallas as pl
from jax.experimental.pallas import tpu as pltpu
from jax.sharding import PartitionSpec as P

PCOLS = 2
STEP = 32
MESH = pl.DeviceIdType.MESH
BF16 = jnp.bfloat16
F32 = jnp.float32


def dft_parts(extent):
    counter = np.arange(extent)
    phases = -2.0 * math.pi / extent * (counter[:, None] * counter[None, :] % extent)
    norm = 1.0 / math.sqrt(extent)
    cosine = (np.cos(phases) * norm).astype(np.float32)
    sine = (np.sin(phases) * norm).astype(np.float32)
    return np.concatenate([cosine, sine], axis=1).astype(jnp.bfloat16)


def dot(left, right):
    return jnp.dot(left, right, preferred_element_type=F32)


def kernel(
    sizes,
    off,
    basis,
    analysis,
    thr,
    dft,
    obj,
    probe,
    mod,
    out_obj,
    out_probe,
    fwd,
    bwd,
    ext,
    power,
    place,
    sum_n,
    sum_d,
    pn,
    pd,
    x_new,
    halo_out,
    halo_in,
    d_out,
    d_in,
    n_out,
    n_in,
    pn_all,
    pd_all,
    a_out,
    a_in,
    b_out,
    b_in,
    halo_sem,
    d_sem,
    n_sem,
    pn_send,
    pn_recv,
    pd_send,
    pd_recv,
    a_send,
    a_recv,
    b_send,
    b_recv,
):
    n_energy, n_mode, n_tile = sizes
    n_chan = n_energy * n_mode
    t = lax.axis_index("tile")
    me = lax.axis_index("energy") * n_mode + lax.axis_index("mode")
    modes, extent = probe.shape[1], probe.shape[2]
    rows, width = obj.shape[1], obj.shape[2]
    positions = mod.shape[0]
    lanes = ext.shape[3]
    pad_w = ext.shape[1] * lanes
    share = rows // n_chan
    comps = thr.shape[0]

    def tile_id(other):
        return {"tile": other}

    def chan_id(other):
        return {"energy": other // n_mode, "mode": other % n_mode}

    barrier = pltpu.get_barrier_semaphore()
    for step in range(1, n_chan):
        pl.semaphore_signal(
            barrier, inc=1, device_id=chan_id((me + step) % n_chan), device_id_type=MESH
        )
    for step in range(1, n_tile):
        pl.semaphore_signal(
            barrier, inc=1, device_id=tile_id((t + step) % n_tile), device_id_type=MESH
        )

    def fill(base, block):
        for start in range(0, width, lanes):
            part = min(lanes, width - start)
            ext[:, start // lanes, base : base + rows, :part] = block[
                :, :, start : start + part
            ].astype(F32)
            if part < lanes:
                ext[:, start // lanes, base : base + rows, part:] = jnp.zeros(
                    (2, rows, lanes - part), F32
                )

    def wide(ref, plane, at):
        return jnp.concatenate(
            [ref[plane, block, at] for block in range(pad_w // lanes)], axis=-1
        )

    rounded = obj[...].astype(BF16)
    halo_out[...] = rounded
    fill(0, rounded)

    pl.semaphore_wait(barrier, n_chan - 1 + n_tile - 1)

    def halo_copy():
        return pltpu.make_async_remote_copy(
            src_ref=halo_out,
            dst_ref=halo_in,
            send_sem=halo_sem.at[0],
            recv_sem=halo_sem.at[1],
            device_id=tile_id((t + n_tile - 1) % n_tile),
            device_id_type=MESH,
        )

    def down_copy(src, dst, sem):
        return pltpu.make_async_remote_copy(
            src_ref=src,
            dst_ref=dst,
            send_sem=sem.at[0],
            recv_sem=sem.at[1],
            device_id=tile_id((t + 1) % n_tile),
            device_id_type=MESH,
        )

    first = t == 0
    last = t == n_tile - 1

    @pl.when(jnp.logical_not(first))
    def _():
        halo_copy().start()

    cosine = dft[:, :extent]
    sine = dft[:, extent:]
    fwd[:extent, :extent] = cosine
    fwd[extent:, extent:] = cosine
    fwd[:extent, extent:] = -sine
    fwd[extent:, :extent] = sine
    bwd[:extent, :extent] = cosine
    bwd[extent:, extent:] = cosine
    bwd[:extent, extent:] = sine
    bwd[extent:, :extent] = -sine

    total = probe[0, 0] * probe[0, 0] + probe[1, 0] * probe[1, 0]
    for m in range(1, modes):
        total += probe[0, m] * probe[0, m] + probe[1, m] * probe[1, m]
    power[...] = total
    floor_d = 0.1 * jnp.max(total) + 1e-06

    place[...] = jnp.zeros_like(place)
    sum_n[...] = jnp.zeros_like(sum_n)
    sum_d[...] = jnp.zeros_like(sum_d)
    pn[...] = jnp.zeros_like(pn)
    pd[...] = jnp.zeros_like(pd)
    span = extent + STEP

    def widen(block, col):
        padded = jnp.concatenate([block, jnp.zeros((extent, pad_w - extent), F32)], axis=1)
        return pltpu.roll(padded, col, axis=1)

    def lay(plane, block, col):
        moved = widen(block, col)
        for start in range(0, pad_w, lanes):
            place[plane, start // lanes, STEP : STEP + extent] = moved[:, start : start + lanes]

    def put_power(q, carry):
        drop = off[q, 0]
        col = STEP * (q % PCOLS) + off[q, 1]
        base = pl.multiple_of(STEP * (q // PCOLS), STEP)
        lay(2, power[...], col)
        sum_d[pl.ds(base, span)] += wide(place, 2, pl.ds(STEP - drop, span))
        return carry

    lax.fori_loop(0, positions, put_power, 0)

    d_out[...] = sum_d[rows:, :width].astype(BF16)

    @pl.when(jnp.logical_not(last))
    def _():
        down_copy(d_out, d_in, d_sem).start()
        halo_copy().wait_recv()
        fill(rows, halo_in[...])

    @pl.when(last)
    def _():
        ext[:, :, rows:] = jnp.zeros((2, pad_w // lanes, rows, lanes), F32)

    def one(q, carry):
        drop = off[q, 0]
        col = STEP * (q % PCOLS) + off[q, 1]
        base = pl.multiple_of(STEP * (q // PCOLS), STEP)
        top = base + drop
        o_r = pltpu.roll(wide(ext, 0, pl.ds(top, extent)), lax.rem(pad_w - col, pad_w), axis=1)[:, :extent]
        o_i = pltpu.roll(wide(ext, 1, pl.ds(top, extent)), lax.rem(pad_w - col, pad_w), axis=1)[:, :extent]
        waves = []
        for m in range(modes):
            p_r, p_i = probe[0, m], probe[1, m]
            waves.append(
                jnp.concatenate([p_r * o_r - p_i * o_i, p_r * o_i + p_i * o_r], axis=0).astype(BF16)
            )
        half = dot(fwd[...], jnp.concatenate(waves, axis=1))
        cols = jnp.concatenate(
            [
                jnp.concatenate(
                    [
                        half[:extent, m * extent : (m + 1) * extent],
                        half[extent:, m * extent : (m + 1) * extent],
                    ],
                    axis=1,
                )
                for m in range(modes)
            ],
            axis=0,
        ).astype(BF16)
        spec = dot(cols, bwd[...])
        parts = [spec[m * extent : (m + 1) * extent] for m in range(modes)]
        squares = parts[0] * parts[0]
        for m in range(1, modes):
            squares += parts[m] * parts[m]
        mag = squares[:, :extent] + squares[:, extent:]
        factor = mod[q].astype(F32) * lax.rsqrt(mag + 0.01)
        both = jnp.concatenate([factor, factor], axis=1)
        scaled = jnp.concatenate([part * both for part in parts], axis=0).astype(BF16)
        ret = dot(scaled, fwd[...])
        stack = jnp.concatenate(
            [
                jnp.concatenate(
                    [
                        ret[m * extent : (m + 1) * extent, :extent],
                        ret[m * extent : (m + 1) * extent, extent:],
                    ],
                    axis=0,
                )
                for m in range(modes)
            ],
            axis=1,
        ).astype(BF16)
        wave = dot(bwd[...], stack)
        n_r = jnp.zeros((extent, extent), F32)
        n_i = jnp.zeros((extent, extent), F32)
        for m in range(modes):
            p_r, p_i = probe[0, m], probe[1, m]
            w_r = wave[:extent, m * extent : (m + 1) * extent]
            w_i = wave[extent:, m * extent : (m + 1) * extent]
            n_r += p_r * w_r + p_i * w_i
            n_i += p_r * w_i - p_i * w_r
            pn[0, m] += o_r * w_r + o_i * w_i
            pn[1, m] += o_r * w_i - o_i * w_r
        pd[...] += o_r * o_r + o_i * o_i
        lay(0, n_r, col)
        lay(1, n_i, col)
        for c in range(2):
            sum_n[c, pl.ds(base, span)] += wide(place, c, pl.ds(STEP - drop, span))
        return carry

    lax.fori_loop(0, positions, one, 0)

    for c in range(2):
        low = sum_n[c, rows:] - sum_d[rows:] * wide(ext, c, slice(rows, None))
        n_out[c] = low[:, :width].astype(BF16)

    @pl.when(jnp.logical_not(last))
    def _():
        down_copy(n_out, n_in, n_sem).start()

    pd_all[t] = pd[...].astype(BF16)
    pn_all[t] = (pn[...] - probe[...] * pd[...]).astype(BF16)

    def probe_copy(buffer, send, recv, step):
        return pltpu.make_async_remote_copy(
            src_ref=buffer.at[t],
            dst_ref=buffer.at[t],
            send_sem=send.at[step - 1],
            recv_sem=recv.at[step - 1],
            device_id=tile_id((t + step) % n_tile),
            device_id_type=MESH,
        )

    for step in range(1, n_tile):
        probe_copy(pd_all, pd_send, pd_recv, step).start()
        probe_copy(pn_all, pn_send, pn_recv, step).start()

    @pl.when(first)
    def _():
        n_in[...] = jnp.zeros_like(n_in)
        d_in[...] = jnp.zeros_like(d_in)

    @pl.when(jnp.logical_not(first))
    def _():
        down_copy(d_out, d_in, d_sem).wait_recv()
        down_copy(n_out, n_in, n_sem).wait_recv()

    d_top = sum_d[:rows, :width]
    n_top = sum_n[:, :rows, :width] - d_top[None] * obj[...].astype(BF16).astype(F32)
    n_top = n_top + n_in[...].astype(F32)
    d_top = d_top + d_in[...].astype(F32)
    fresh = obj[...] + n_top / (d_top + floor_d)[None]
    x_new[...] = fresh

    for block in range(n_chan):
        a_out[block, :, :share] = fresh[:, block * share : (block + 1) * share].astype(BF16)
    a_in[me] = a_out[me]

    def chan_copy(src, dst, send, recv, step):
        other = (me + step) % n_chan
        return pltpu.make_async_remote_copy(
            src_ref=src.at[other],
            dst_ref=dst.at[me],
            send_sem=send.at[step - 1],
            recv_sem=recv.at[step - 1],
            device_id=chan_id(other),
            device_id_type=MESH,
        )

    for step in range(1, n_chan):
        chan_copy(a_out, a_in, a_send, a_recv, step).start()
    for step in range(1, n_chan):
        chan_copy(a_out, a_in, a_send, a_recv, step).wait_recv()

    spectra = [a_in[e].astype(F32) for e in range(n_chan)]
    shrunk = []
    for k in range(comps):
        c = analysis[k, 0] * spectra[0]
        for e in range(1, n_chan):
            c += analysis[k, e] * spectra[e]
        limit = thr[k]
        shrunk.append(c - jnp.minimum(jnp.maximum(c, -limit), limit))
    for e in range(n_chan):
        x = basis[e, 0] * shrunk[0]
        for k in range(1, comps):
            x += basis[e, k] * shrunk[k]
        b_out[e] = x.astype(BF16)
    b_in[me] = b_out[me]

    for step in range(1, n_chan):
        chan_copy(b_out, b_in, b_send, b_recv, step).start()

    for step in range(1, n_tile):
        probe_copy(pd_all, pd_send, pd_recv, step).wait_recv()
        probe_copy(pn_all, pn_send, pn_recv, step).wait_recv()
    den = pd_all[0].astype(F32)
    num = pn_all[0].astype(F32)
    for other in range(1, n_tile):
        den += pd_all[other].astype(F32)
        num += pn_all[other].astype(F32)
    out_probe[...] = probe[...] + num / (den + 0.1 * jnp.max(den) + 1e-06)

    for step in range(1, n_chan):
        chan_copy(b_out, b_in, b_send, b_recv, step).wait_recv()
    for block in range(n_chan):
        at = slice(block * share, (block + 1) * share)
        out_obj[:, at] = 0.5 * x_new[:, at] + 0.5 * b_in[block, :, :share].astype(F32)

    @pl.when(jnp.logical_not(first))
    def _():
        halo_copy().wait_send()

    @pl.when(jnp.logical_not(last))
    def _():
        down_copy(d_out, d_in, d_sem).wait_send()
        down_copy(n_out, n_in, n_sem).wait_send()

    for step in range(1, n_tile):
        probe_copy(pd_all, pd_send, pd_recv, step).wait_send()
        probe_copy(pn_all, pn_send, pn_recv, step).wait_send()
    for step in range(1, n_chan):
        chan_copy(a_out, a_in, a_send, a_recv, step).wait_send()
        chan_copy(b_out, b_in, b_send, b_recv, step).wait_send()


def body(sizes, object_field, probe_field, modulus, offsets, spectra_basis, analysis, threshold):
    n_energy, n_mode, n_tile = sizes
    n_chan = n_energy * n_mode
    extent = probe_field.shape[-1]
    modes = probe_field.shape[1]
    rows, width = object_field.shape[2:]
    pad_w = -(-width // 128) * 128
    share = max(16, rows // n_chan)
    positions = offsets.shape[0]
    vmem = pl.BlockSpec(memory_space=pltpu.VMEM)
    smem = pl.BlockSpec(memory_space=pltpu.SMEM)
    dma = pltpu.SemaphoreType.DMA
    peers = max(1, n_tile - 1)
    flops = positions * modes * 4 * 2 * (2 * extent) ** 2 * extent
    out_obj, out_probe = pl.pallas_call(
        functools.partial(kernel, sizes),
        out_shape=(
            jax.ShapeDtypeStruct((2, rows, width), F32),
            jax.ShapeDtypeStruct((2, modes, extent, extent), F32),
        ),
        in_specs=[smem] * 4 + [vmem] * 4,
        out_specs=(vmem, vmem),
        scratch_shapes=[
            pltpu.VMEM((2 * extent, 2 * extent), BF16),
            pltpu.VMEM((2 * extent, 2 * extent), BF16),
            pltpu.VMEM((2, pad_w // 128, 2 * rows, 128), F32),
            pltpu.VMEM((extent, extent), F32),
            pltpu.VMEM((3, pad_w // 128, extent + 2 * STEP, 128), F32),
            pltpu.VMEM((2, 2 * rows, pad_w), F32),
            pltpu.VMEM((2 * rows, pad_w), F32),
            pltpu.VMEM((2, modes, extent, extent), F32),
            pltpu.VMEM((extent, extent), F32),
            pltpu.VMEM((2, rows, width), F32),
            pltpu.VMEM((2, rows, width), BF16),
            pltpu.VMEM((2, rows, width), BF16),
            pltpu.VMEM((rows, width), BF16),
            pltpu.VMEM((rows, width), BF16),
            pltpu.VMEM((2, rows, width), BF16),
            pltpu.VMEM((2, rows, width), BF16),
            pltpu.VMEM((n_tile, 2, modes, extent, extent), BF16),
            pltpu.VMEM((n_tile, extent, extent), BF16),
            pltpu.VMEM((n_chan, 2, share, width), BF16),
            pltpu.VMEM((n_chan, 2, share, width), BF16),
            pltpu.VMEM((n_chan, 2, share, width), BF16),
            pltpu.VMEM((n_chan, 2, share, width), BF16),
            dma((2,)),
            dma((2,)),
            dma((2,)),
            dma((peers,)),
            dma((peers,)),
            dma((peers,)),
            dma((peers,)),
            dma((n_chan - 1,)),
            dma((n_chan - 1,)),
            dma((n_chan - 1,)),
            dma((n_chan - 1,)),
        ],
        compiler_params=pltpu.CompilerParams(
            collective_id=0, has_side_effects=True, vmem_limit_bytes=40 * 1024 * 1024
        ),
        cost_estimate=pl.CostEstimate(flops=flops, bytes_accessed=2000000, transcendentals=0),
    )(
        offsets,
        spectra_basis,
        analysis,
        threshold,
        jnp.asarray(dft_parts(extent)),
        object_field.reshape(2, rows, width),
        probe_field.reshape(2, modes, extent, extent),
        modulus.reshape(positions, extent, extent),
    )
    return (out_obj[:, None], out_probe[:, :, None])


def solution(mesh):
    sizes = (mesh.shape["energy"], mesh.shape["mode"], mesh.shape["tile"])
    placed = (
        P(None, ("groups", "energy", "mode"), "tile", None),
        P(None, None, ("groups", "energy", "mode"), None, None),
        P(("groups", "energy", "mode"), "tile", None, None),
        P(("groups", "tile"), None),
        P(),
        P(),
        P(),
    )
    return jax.shard_map(
        functools.partial(body, sizes),
        mesh=mesh,
        in_specs=placed,
        out_specs=(
            P(None, ("groups", "energy", "mode"), "tile", None),
            P(None, None, ("groups", "energy", "mode"), None, None),
        ),
        check_vma=False,
    )
```

```python
import functools
import math

import jax
import jax.numpy as jnp
import numpy as np
from jax import lax
from jax.experimental import pallas as pl
from jax.experimental.pallas import tpu as pltpu
from jax.sharding import PartitionSpec as P

PCOLS = 2
STEP = 32
MESH = pl.DeviceIdType.MESH
BF16 = jnp.bfloat16
F32 = jnp.float32


def dft_parts(extent):
    counter = np.arange(extent)
    phases = -2.0 * math.pi / extent * (counter[:, None] * counter[None, :] % extent)
    norm = 1.0 / math.sqrt(extent)
    cosine = (np.cos(phases) * norm).astype(np.float32)
    sine = (np.sin(phases) * norm).astype(np.float32)
    return np.concatenate([cosine, sine], axis=1).astype(jnp.bfloat16)


def dot(left, right):
    return jnp.dot(left, right, preferred_element_type=F32)


def kernel(
    sizes,
    off_hbm,
    basis_hbm,
    analysis_hbm,
    thr_hbm,
    dft_hbm,
    obj_hbm,
    probe_hbm,
    mod_hbm,
    out_obj,
    out_probe,
    off,
    basis,
    analysis,
    thr,
    dft,
    obj,
    probe,
    mod,
    load_sem,
    fwd,
    bwd,
    probe_t,
    ext,
    power,
    place,
    sum_n,
    sum_d,
    pn,
    pd,
    halo_out,
    halo_in,
    d_out,
    d_in,
    n_out,
    n_in,
    pn_all,
    pd_all,
    x_new,
    a_out,
    a_in,
    b_out,
    b_in,
    halo_sem,
    d_sem,
    n_sem,
    pn_send,
    pn_recv,
    pd_send,
    pd_recv,
    a_send,
    a_recv,
    b_send,
    b_recv,
):
    n_energy, n_mode, n_tile = sizes
    n_chan = n_energy * n_mode
    t = lax.axis_index("tile")
    me = lax.axis_index("energy") * n_mode + lax.axis_index("mode")
    modes, extent = probe.shape[1], probe.shape[2]
    width, rows = obj.shape[1], obj.shape[2]
    positions = mod.shape[0]
    share = width // n_chan
    used = 2 * share
    comps = thr.shape[0]

    def tile_id(other):
        return {"tile": other}

    def chan_id(other):
        return {"energy": other // n_mode, "mode": other % n_mode}

    barrier = pltpu.get_barrier_semaphore()
    for step in range(1, n_chan):
        pl.semaphore_signal(
            barrier, inc=1, device_id=chan_id((me + step) % n_chan), device_id_type=MESH
        )
    for step in range(1, n_tile):
        pl.semaphore_signal(
            barrier, inc=1, device_id=tile_id((t + step) % n_tile), device_id_type=MESH
        )

    pairs = [
        (obj_hbm, obj),
        (off_hbm, off),
        (probe_hbm, probe),
        (dft_hbm, dft),
        (mod_hbm, mod),
        (analysis_hbm, analysis),
        (basis_hbm, basis),
        (thr_hbm, thr),
    ]
    loads = [
        pltpu.make_async_copy(src, dst, load_sem.at[i]) for i, (src, dst) in enumerate(pairs)
    ]
    for load in loads:
        load.start()

    place[...] = jnp.zeros_like(place)
    sum_n[...] = jnp.zeros_like(sum_n)
    sum_d[...] = jnp.zeros_like(sum_d)
    pn[...] = jnp.zeros_like(pn)
    pd[...] = jnp.zeros_like(pd)

    loads[0].wait()
    rounded = obj[...].astype(BF16)
    halo_out[...] = rounded
    ext[:, 0] = rounded.astype(F32)

    pl.semaphore_wait(barrier, n_chan - 1 + n_tile - 1)

    def halo_copy():
        return pltpu.make_async_remote_copy(
            src_ref=halo_out,
            dst_ref=halo_in,
            send_sem=halo_sem.at[0],
            recv_sem=halo_sem.at[1],
            device_id=tile_id((t + n_tile - 1) % n_tile),
            device_id_type=MESH,
        )

    def down_copy(src, dst, sem):
        return pltpu.make_async_remote_copy(
            src_ref=src,
            dst_ref=dst,
            send_sem=sem.at[0],
            recv_sem=sem.at[1],
            device_id=tile_id((t + 1) % n_tile),
            device_id_type=MESH,
        )

    first = t == 0
    last = t == n_tile - 1

    @pl.when(jnp.logical_not(first))
    def _():
        halo_copy().start()

    loads[2].wait()
    total = jnp.zeros((extent, extent), F32)
    for m in range(modes):
        for c in range(2):
            turned = probe[c, m].T
            probe_t[c, m] = turned
            total += turned * turned
    power[...] = total
    floor_d = 0.1 * jnp.max(total) + 1e-06
    span = extent + STEP

    def lay(plane, block, row):
        moved = pltpu.roll(
            jnp.concatenate([block, jnp.zeros((extent, rows), F32)], axis=1), row, axis=1
        )
        place[plane, 0, STEP : STEP + extent] = moved[:, :rows]
        place[plane, 1, STEP : STEP + extent] = moved[:, rows:]

    loads[1].wait()

    def put_power(k, carry):
        for c in range(PCOLS):
            q = k * PCOLS + c
            lay(c, power[...], STEP * k + off[0, q])
            for b in range(2):
                sum_d[b, STEP * c : STEP * c + span] += place[
                    c, b, pl.ds(STEP - off[1, q], span)
                ]
        return carry

    lax.fori_loop(0, positions // PCOLS, put_power, 0)

    d_out[...] = sum_d[1].astype(BF16)

    loads[3].wait()
    cosine = dft[:, :extent]
    sine = dft[:, extent:]
    fwd[:extent, :extent] = cosine
    fwd[extent:, extent:] = cosine
    fwd[:extent, extent:] = -sine
    fwd[extent:, :extent] = sine
    bwd[:extent, :extent] = cosine
    bwd[extent:, extent:] = cosine
    bwd[:extent, extent:] = sine
    bwd[extent:, :extent] = -sine
    loads[4].wait()

    @pl.when(jnp.logical_not(last))
    def _():
        down_copy(d_out, d_in, d_sem).start()
        halo_copy().wait_recv()
        ext[:, 1] = halo_in[...].astype(F32)

    @pl.when(last)
    def _():
        ext[:, 1] = jnp.zeros((2, width, rows), F32)

    def window(plane, row, col):
        both = jnp.concatenate(
            [ext[plane, b, pl.ds(col, extent)] for b in range(2)], axis=1
        )
        return pltpu.roll(both, lax.rem(2 * rows - row, 2 * rows), axis=1)[:, :extent]

    def lanes_of(array, index):
        return array[:, index * extent : (index + 1) * extent]

    def rows_of(array, index):
        return array[index * extent : (index + 1) * extent]

    def one(k, carry):
        objects, tall = [], []
        for c in range(PCOLS):
            q = k * PCOLS + c
            row, col = STEP * k + off[0, q], STEP * c + off[1, q]
            o_r, o_i = window(0, row, col), window(1, row, col)
            objects.append((o_r, o_i))
            for m in range(modes):
                p_r, p_i = probe_t[0, m], probe_t[1, m]
                tall.append(
                    jnp.concatenate(
                        [p_r * o_r - p_i * o_i, p_r * o_i + p_i * o_r], axis=1
                    ).astype(BF16)
                )
        n_c = []
        for c in range(PCOLS):
            half = dot(jnp.concatenate(tall[c * modes : (c + 1) * modes], axis=0), bwd[...])
            wide = jnp.concatenate(
                [
                    jnp.concatenate(
                        [rows_of(half, m)[:, :extent], rows_of(half, m)[:, extent:]], axis=0
                    )
                    for m in range(modes)
                ],
                axis=1,
            ).astype(BF16)
            spec = dot(fwd[...], wide)
            squares = lanes_of(spec, 0) * lanes_of(spec, 0)
            for m in range(1, modes):
                squares += lanes_of(spec, m) * lanes_of(spec, m)
            mag = squares[:extent] + squares[extent:]
            factor = mod[k * PCOLS + c].astype(F32).T * lax.rsqrt(mag + 0.01)
            both = jnp.concatenate([factor, factor], axis=0)
            scaled = jnp.concatenate(
                [(lanes_of(spec, m) * both).astype(BF16) for m in range(modes)], axis=1
            )
            ret = dot(bwd[...], scaled)
            cols = jnp.concatenate(
                [
                    jnp.concatenate(
                        [lanes_of(ret, m)[:extent], lanes_of(ret, m)[extent:]], axis=1
                    )
                    for m in range(modes)
                ],
                axis=0,
            ).astype(BF16)
            wave = dot(cols, fwd[...])
            o_r, o_i = objects[c]
            n_r = jnp.zeros((extent, extent), F32)
            n_i = jnp.zeros((extent, extent), F32)
            for m in range(modes):
                p_r, p_i = probe_t[0, m], probe_t[1, m]
                w_r, w_i = rows_of(wave, m)[:, :extent], rows_of(wave, m)[:, extent:]
                n_r += p_r * w_r + p_i * w_i
                n_i += p_r * w_i - p_i * w_r
                pn[0, m] += o_r * w_r + o_i * w_i
                pn[1, m] += o_r * w_i - o_i * w_r
            pd[...] += o_r * o_r + o_i * o_i
            n_c.append((n_r, n_i))
        for c in range(PCOLS):
            q = k * PCOLS + c
            for plane in range(2):
                lay(2 * c + plane, n_c[c][plane], STEP * k + off[0, q])
        for c in range(PCOLS):
            q = k * PCOLS + c
            for plane in range(2):
                for b in range(2):
                    sum_n[plane, b, STEP * c : STEP * c + span] += place[
                        2 * c + plane, b, pl.ds(STEP - off[1, q], span)
                    ]
        return carry

    lax.fori_loop(0, positions // PCOLS, one, 0)

    for plane in range(2):
        n_out[plane] = (sum_n[plane, 1] - sum_d[1] * ext[plane, 1]).astype(BF16)

    @pl.when(jnp.logical_not(last))
    def _():
        down_copy(n_out, n_in, n_sem).start()

    pd_all[t] = pd[...].astype(BF16)
    pn_all[t] = (pn[...] - probe_t[...] * pd[...]).astype(BF16)

    def probe_copy(buffer, send, recv, step):
        return pltpu.make_async_remote_copy(
            src_ref=buffer.at[t],
            dst_ref=buffer.at[t],
            send_sem=send.at[step - 1],
            recv_sem=recv.at[step - 1],
            device_id=tile_id((t + step) % n_tile),
            device_id_type=MESH,
        )

    for step in range(1, n_tile):
        probe_copy(pd_all, pd_send, pd_recv, step).start()
        probe_copy(pn_all, pn_send, pn_recv, step).start()

    @pl.when(first)
    def _():
        n_in[...] = jnp.zeros_like(n_in)
        d_in[...] = jnp.zeros_like(d_in)

    @pl.when(jnp.logical_not(first))
    def _():
        down_copy(d_out, d_in, d_sem).wait_recv()
        down_copy(n_out, n_in, n_sem).wait_recv()

    scale = 1.0 / (sum_d[0] + d_in[...].astype(F32) + floor_d)
    for plane in range(2):
        top = sum_n[plane, 0] - sum_d[0] * ext[plane, 0] + n_in[plane].astype(F32)
        x_new[plane] = obj[plane] + top * scale

    for block in range(n_chan):
        at = slice(block * share, (block + 1) * share)
        a_out[block, :used] = jnp.concatenate([x_new[0, at], x_new[1, at]], axis=0).astype(BF16)

    def chan_copy(src, dst, send, recv, step):
        other = (me + step) % n_chan
        return pltpu.make_async_remote_copy(
            src_ref=src.at[other],
            dst_ref=dst.at[me],
            send_sem=send.at[step - 1],
            recv_sem=recv.at[step - 1],
            device_id=chan_id(other),
            device_id_type=MESH,
        )

    for step in range(1, n_chan):
        chan_copy(a_out, a_in, a_send, a_recv, step).start()
    a_in[me] = a_out[me]
    for i in range(5, 8):
        loads[i].wait()
    for step in range(1, n_chan):
        chan_copy(a_out, a_in, a_send, a_recv, step).wait_recv()

    spectra = [a_in[e].astype(F32) for e in range(n_chan)]
    shrunk = []
    for k in range(comps):
        c = analysis[k, 0] * spectra[0]
        for e in range(1, n_chan):
            c += analysis[k, e] * spectra[e]
        limit = thr[k]
        shrunk.append(c - jnp.minimum(jnp.maximum(c, -limit), limit))
    for e in range(n_chan):
        x = basis[e, 0] * shrunk[0]
        for k in range(1, comps):
            x += basis[e, k] * shrunk[k]
        b_out[e] = x.astype(BF16)

    for step in range(1, n_chan):
        chan_copy(b_out, b_in, b_send, b_recv, step).start()
    b_in[me] = b_out[me]

    for step in range(1, n_tile):
        probe_copy(pd_all, pd_send, pd_recv, step).wait_recv()
        probe_copy(pn_all, pn_send, pn_recv, step).wait_recv()
    den = pd_all[0].astype(F32)
    for other in range(1, n_tile):
        den += pd_all[other].astype(F32)
    scale = 1.0 / (den + 0.1 * jnp.max(den) + 1e-06)
    for c in range(2):
        for m in range(modes):
            num = pn_all[0, c, m].astype(F32)
            for other in range(1, n_tile):
                num += pn_all[other, c, m].astype(F32)
            out_probe[c, m] = probe[c, m] + (num * scale).T

    for step in range(1, n_chan):
        chan_copy(b_out, b_in, b_send, b_recv, step).wait_recv()
    for block in range(n_chan):
        at = slice(block * share, (block + 1) * share)
        back = b_in[block].astype(F32)
        out_obj[0, at] = 0.5 * x_new[0, at] + 0.5 * back[:share]
        out_obj[1, at] = 0.5 * x_new[1, at] + 0.5 * back[share:used]

    @pl.when(jnp.logical_not(first))
    def _():
        halo_copy().wait_send()

    @pl.when(jnp.logical_not(last))
    def _():
        down_copy(d_out, d_in, d_sem).wait_send()
        down_copy(n_out, n_in, n_sem).wait_send()

    for step in range(1, n_tile):
        probe_copy(pd_all, pd_send, pd_recv, step).wait_send()
        probe_copy(pn_all, pn_send, pn_recv, step).wait_send()
    for step in range(1, n_chan):
        chan_copy(a_out, a_in, a_send, a_recv, step).wait_send()
        chan_copy(b_out, b_in, b_send, b_recv, step).wait_send()


def body(sizes, object_field, probe_field, modulus, offsets, spectra_basis, analysis, threshold):
    n_energy, n_mode, n_tile = sizes
    n_chan = n_energy * n_mode
    extent = probe_field.shape[-1]
    modes = probe_field.shape[1]
    rows, width = object_field.shape[2:]
    share = -(-2 * (width // n_chan) // 16) * 16
    positions = offsets.shape[0]
    hbm = pl.BlockSpec(memory_space=pltpu.HBM)
    vmem = pl.BlockSpec(memory_space=pltpu.VMEM)
    dma = pltpu.SemaphoreType.DMA
    peers = max(1, n_tile - 1)
    flops = positions * modes * 4 * 2 * (2 * extent) ** 2 * extent
    dft = dft_parts(extent)
    out_obj, out_probe = pl.pallas_call(
        functools.partial(kernel, sizes),
        out_shape=(
            jax.ShapeDtypeStruct((2, width, rows), F32),
            jax.ShapeDtypeStruct((2, modes, extent, extent), F32),
        ),
        in_specs=[hbm] * 8,
        out_specs=(vmem, vmem),
        scratch_shapes=[
            pltpu.SMEM(offsets.shape[::-1], jnp.int32),
            pltpu.SMEM(spectra_basis.shape, F32),
            pltpu.SMEM(analysis.shape, F32),
            pltpu.SMEM(threshold.shape, F32),
            pltpu.VMEM(dft.shape, BF16),
            pltpu.VMEM((2, width, rows), F32),
            pltpu.VMEM((2, modes, extent, extent), F32),
            pltpu.VMEM((positions, extent, extent), BF16),
            dma((8,)),
            pltpu.VMEM((2 * extent, 2 * extent), BF16),
            pltpu.VMEM((2 * extent, 2 * extent), BF16),
            pltpu.VMEM((2, modes, extent, extent), F32),
            pltpu.VMEM((2, 2, width, rows), F32),
            pltpu.VMEM((extent, extent), F32),
            pltpu.VMEM((2 * PCOLS, 2, extent + 2 * STEP, rows), F32),
            pltpu.VMEM((2, 2, width, rows), F32),
            pltpu.VMEM((2, width, rows), F32),
            pltpu.VMEM((2, modes, extent, extent), F32),
            pltpu.VMEM((extent, extent), F32),
            pltpu.VMEM((2, width, rows), BF16),
            pltpu.VMEM((2, width, rows), BF16),
            pltpu.VMEM((width, rows), BF16),
            pltpu.VMEM((width, rows), BF16),
            pltpu.VMEM((2, width, rows), BF16),
            pltpu.VMEM((2, width, rows), BF16),
            pltpu.VMEM((n_tile, 2, modes, extent, extent), BF16),
            pltpu.VMEM((n_tile, extent, extent), BF16),
            pltpu.VMEM((2, width, rows), F32),
            pltpu.VMEM((n_chan, share, rows), BF16),
            pltpu.VMEM((n_chan, share, rows), BF16),
            pltpu.VMEM((n_chan, share, rows), BF16),
            pltpu.VMEM((n_chan, share, rows), BF16),
            dma((2,)),
            dma((2,)),
            dma((2,)),
            dma((peers,)),
            dma((peers,)),
            dma((peers,)),
            dma((peers,)),
            dma((n_chan - 1,)),
            dma((n_chan - 1,)),
            dma((n_chan - 1,)),
            dma((n_chan - 1,)),
        ],
        compiler_params=pltpu.CompilerParams(
            collective_id=0, has_side_effects=True, vmem_limit_bytes=40 * 1024 * 1024
        ),
        cost_estimate=pl.CostEstimate(flops=flops, bytes_accessed=2000000, transcendentals=0),
    )(
        offsets.T,
        spectra_basis,
        analysis,
        threshold,
        jnp.asarray(dft),
        jnp.swapaxes(object_field, 2, 3).reshape(2, width, rows),
        probe_field.reshape(2, modes, extent, extent),
        modulus.reshape(positions, extent, extent),
    )
    return (jnp.swapaxes(out_obj, 1, 2)[:, None], out_probe[:, :, None])


def solution(mesh):
    sizes = (mesh.shape["energy"], mesh.shape["mode"], mesh.shape["tile"])
    placed = (
        P(None, ("groups", "energy", "mode"), "tile", None),
        P(None, None, ("groups", "energy", "mode"), None, None),
        P(("groups", "energy", "mode"), "tile", None, None),
        P(("groups", "tile"), None),
        P(),
        P(),
        P(),
    )
    return jax.shard_map(
        functools.partial(body, sizes),
        mesh=mesh,
        in_specs=placed,
        out_specs=(
            P(None, ("groups", "energy", "mode"), "tile", None),
            P(None, None, ("groups", "energy", "mode"), None, None),
        ),
        check_vma=False,
    )
```

```python
import functools
import math

import jax
import jax.numpy as jnp
import numpy as np
from jax import lax
from jax.experimental import pallas as pl
from jax.experimental.pallas import tpu as pltpu
from jax.sharding import PartitionSpec as P

PCOLS = 2
STEP = 32
MESH = pl.DeviceIdType.MESH
BF16 = jnp.bfloat16
F32 = jnp.float32


def dft_parts(extent):
    counter = np.arange(extent)
    phases = -2.0 * math.pi / extent * (counter[:, None] * counter[None, :] % extent)
    norm = 1.0 / math.sqrt(extent)
    cosine = (np.cos(phases) * norm).astype(np.float32)
    sine = (np.sin(phases) * norm).astype(np.float32)
    return np.concatenate([cosine, sine], axis=1).astype(jnp.bfloat16)


def dot(left, right):
    return jnp.dot(left, right, preferred_element_type=F32)


def kernel(
    sizes,
    off_hbm,
    basis_hbm,
    analysis_hbm,
    thr_hbm,
    dft_hbm,
    obj_hbm,
    probe_hbm,
    mod_hbm,
    out_obj,
    out_probe,
    off,
    basis,
    analysis,
    thr,
    dft,
    obj,
    probe,
    mod,
    load_sem,
    fwd,
    bwd,
    probe_t,
    ext,
    power,
    place,
    sum_n,
    sum_d,
    pn,
    pd,
    halo_out,
    halo_in,
    d_out,
    d_in,
    n_out,
    n_in,
    rest_out,
    rest_in,
    pn_all,
    pd_all,
    x_new,
    a_out,
    a_in,
    b_out,
    b_in,
    halo_sem,
    d_sem,
    n_sem,
    pn_send,
    pn_recv,
    pd_send,
    pd_recv,
    a_send,
    a_recv,
    b_send,
    b_recv,
):
    n_energy, n_mode, n_tile = sizes
    n_chan = n_energy * n_mode
    t = lax.axis_index("tile")
    me = lax.axis_index("energy") * n_mode + lax.axis_index("mode")
    modes, extent = probe.shape[1], probe.shape[2]
    width, rows = obj.shape[1], obj.shape[2]
    positions = mod.shape[0]
    share = width // n_chan
    used = 2 * share
    comps = thr.shape[0]

    def tile_id(other):
        return {"tile": other}

    def chan_id(other):
        return {"energy": other // n_mode, "mode": other % n_mode}

    barrier = pltpu.get_barrier_semaphore()
    for step in range(1, n_chan):
        pl.semaphore_signal(
            barrier, inc=1, device_id=chan_id((me + step) % n_chan), device_id_type=MESH
        )
    for step in range(1, n_tile):
        pl.semaphore_signal(
            barrier, inc=1, device_id=tile_id((t + step) % n_tile), device_id_type=MESH
        )

    pairs = [
        (obj_hbm, obj),
        (off_hbm, off),
        (probe_hbm, probe),
        (dft_hbm, dft),
        (mod_hbm, mod),
        (analysis_hbm, analysis),
        (basis_hbm, basis),
        (thr_hbm, thr),
    ]
    loads = [
        pltpu.make_async_copy(src, dst, load_sem.at[i]) for i, (src, dst) in enumerate(pairs)
    ]
    for load in loads:
        load.start()

    place[...] = jnp.zeros_like(place)
    sum_n[...] = jnp.zeros_like(sum_n)
    sum_d[...] = jnp.zeros_like(sum_d)
    pn[...] = jnp.zeros_like(pn)
    pd[...] = jnp.zeros_like(pd)

    loads[0].wait()
    near, fold = width // 2, rows // 2
    for part in range(2):
        halo_out[part] = jnp.concatenate(
            [
                obj[:, :near, part * fold : (part + 1) * fold],
                obj[:, near:, part * fold : (part + 1) * fold],
            ],
            axis=2,
        ).astype(BF16)
    ext[:, 0] = obj[...].astype(BF16).astype(F32)

    pl.semaphore_wait(barrier, n_chan - 1 + n_tile - 1)

    def halo_copy(part):
        return pltpu.make_async_remote_copy(
            src_ref=halo_out.at[part],
            dst_ref=halo_in.at[part],
            send_sem=halo_sem.at[part],
            recv_sem=halo_sem.at[2 + part],
            device_id=tile_id((t + n_tile - 1) % n_tile),
            device_id_type=MESH,
        )

    def down_copy(src, dst, send, recv):
        return pltpu.make_async_remote_copy(
            src_ref=src,
            dst_ref=dst,
            send_sem=send,
            recv_sem=recv,
            device_id=tile_id((t + 1) % n_tile),
            device_id_type=MESH,
        )

    first = t == 0
    last = t == n_tile - 1

    @pl.when(jnp.logical_not(first))
    def _():
        halo_copy(0).start()
        halo_copy(1).start()

    loads[2].wait()
    total = jnp.zeros((extent, extent), F32)
    for m in range(modes):
        for c in range(2):
            turned = probe[c, m].T
            probe_t[c, m] = turned
            total += turned * turned
    power[...] = total
    floor_d = 0.1 * jnp.max(total) + 1e-06
    span = extent + STEP

    def lay(plane, block, row):
        moved = pltpu.roll(
            jnp.concatenate([block, jnp.zeros((extent, rows), F32)], axis=1), row, axis=1
        )
        place[plane, 0, STEP : STEP + extent] = moved[:, :rows]
        place[plane, 1, STEP : STEP + extent] = moved[:, rows:]

    loads[1].wait()

    def put_power(k, carry):
        for c in range(PCOLS):
            q = k * PCOLS + c
            lay(c, power[...], STEP * k + off[0, q])
            for b in range(2):
                sum_d[b, STEP * c : STEP * c + span] += place[
                    c, b, pl.ds(STEP - off[1, q], span)
                ]
        return carry

    lax.fori_loop(0, positions // PCOLS, put_power, 0)

    d_out[...] = sum_d[1].astype(BF16)

    loads[3].wait()
    cosine = dft[:, :extent]
    sine = dft[:, extent:]
    fwd[:extent, :extent] = cosine
    fwd[extent:, extent:] = cosine
    fwd[:extent, extent:] = -sine
    fwd[extent:, :extent] = sine
    bwd[:extent, :extent] = cosine
    bwd[extent:, extent:] = cosine
    bwd[:extent, extent:] = sine
    bwd[extent:, :extent] = -sine
    loads[4].wait()

    def take_halo(part):
        halo_copy(part).wait_recv()
        packed = halo_in[part].astype(F32)
        ext[:, 1, :near, part * fold : (part + 1) * fold] = packed[:, :, :fold]
        ext[:, 1, near:, part * fold : (part + 1) * fold] = packed[:, :, fold:]

    @pl.when(jnp.logical_not(last))
    def _():
        down_copy(d_out, d_in, d_sem.at[0], d_sem.at[1]).start()
        take_halo(0)

    @pl.when(last)
    def _():
        ext[:, 1] = jnp.zeros((2, width, rows), F32)

    def window(plane, row, col):
        both = jnp.concatenate(
            [ext[plane, b, pl.ds(col, extent)] for b in range(2)], axis=1
        )
        return pltpu.roll(both, lax.rem(2 * rows - row, 2 * rows), axis=1)[:, :extent]

    def lanes_of(array, index):
        return array[:, index * extent : (index + 1) * extent]

    def rows_of(array, index):
        return array[index * extent : (index + 1) * extent]

    turns = positions // PCOLS
    group = width // (rows // STEP)

    def send_most():
        for plane in range(2):
            n_out[plane] = (sum_n[plane, 1] - sum_d[1] * ext[plane, 1]).astype(BF16)
            sum_n[plane, 1] = jnp.zeros((width, rows), F32)

        @pl.when(jnp.logical_not(last))
        def _():
            down_copy(n_out, n_in, n_sem.at[0], n_sem.at[1]).start()

    def one(i, carry):
        k = lax.rem(i + 1, turns)

        @pl.when(jnp.logical_and(i == 1, jnp.logical_not(last)))
        def _():
            take_halo(1)

        @pl.when(i == turns - 1)
        def _():
            send_most()

        objects, tall = [], []
        for c in range(PCOLS):
            q = k * PCOLS + c
            row, col = STEP * k + off[0, q], STEP * c + off[1, q]
            o_r, o_i = window(0, row, col), window(1, row, col)
            objects.append((o_r, o_i))
            for m in range(modes):
                p_r, p_i = probe_t[0, m], probe_t[1, m]
                tall.append(
                    jnp.concatenate(
                        [p_r * o_r - p_i * o_i, p_r * o_i + p_i * o_r], axis=1
                    ).astype(BF16)
                )
        n_c = []
        for c in range(PCOLS):
            half = dot(jnp.concatenate(tall[c * modes : (c + 1) * modes], axis=0), bwd[...])
            wide = jnp.concatenate(
                [
                    jnp.concatenate(
                        [rows_of(half, m)[:, :extent], rows_of(half, m)[:, extent:]], axis=0
                    )
                    for m in range(modes)
                ],
                axis=1,
            ).astype(BF16)
            spec = dot(fwd[...], wide)
            squares = lanes_of(spec, 0) * lanes_of(spec, 0)
            for m in range(1, modes):
                squares += lanes_of(spec, m) * lanes_of(spec, m)
            mag = squares[:extent] + squares[extent:]
            factor = mod[k * PCOLS + c].astype(F32).T * lax.rsqrt(mag + 0.01)
            both = jnp.concatenate([factor, factor], axis=0)
            scaled = jnp.concatenate(
                [(lanes_of(spec, m) * both).astype(BF16) for m in range(modes)], axis=1
            )
            ret = dot(bwd[...], scaled)
            cols = jnp.concatenate(
                [
                    jnp.concatenate(
                        [lanes_of(ret, m)[:extent], lanes_of(ret, m)[extent:]], axis=1
                    )
                    for m in range(modes)
                ],
                axis=0,
            ).astype(BF16)
            wave = dot(cols, fwd[...])
            o_r, o_i = objects[c]
            n_r = jnp.zeros((extent, extent), F32)
            n_i = jnp.zeros((extent, extent), F32)
            for m in range(modes):
                p_r, p_i = probe_t[0, m], probe_t[1, m]
                w_r, w_i = rows_of(wave, m)[:, :extent], rows_of(wave, m)[:, extent:]
                n_r += p_r * w_r + p_i * w_i
                n_i += p_r * w_i - p_i * w_r
                pn[0, m] += o_r * w_r + o_i * w_i
                pn[1, m] += o_r * w_i - o_i * w_r
            pd[...] += o_r * o_r + o_i * o_i
            n_c.append((n_r, n_i))
        for c in range(PCOLS):
            q = k * PCOLS + c
            for plane in range(2):
                lay(2 * c + plane, n_c[c][plane], STEP * k + off[0, q])
        for c in range(PCOLS):
            q = k * PCOLS + c
            for plane in range(2):
                for b in range(2):
                    sum_n[plane, b, STEP * c : STEP * c + span] += place[
                        2 * c + plane, b, pl.ds(STEP - off[1, q], span)
                    ]
        return carry

    lax.fori_loop(0, turns, one, 0)

    for plane in range(2):
        rest_out[plane] = jnp.concatenate(
            [
                sum_n[plane, 1, g * group : (g + 1) * group, :STEP]
                for g in range(rows // STEP)
            ],
            axis=1,
        ).astype(BF16)

    @pl.when(jnp.logical_not(last))
    def _():
        down_copy(rest_out, rest_in, n_sem.at[2], n_sem.at[3]).start()

    @pl.when(first)
    def _():
        n_in[...] = jnp.zeros_like(n_in)
        rest_in[...] = jnp.zeros_like(rest_in)
        d_in[...] = jnp.zeros_like(d_in)

    @pl.when(jnp.logical_not(first))
    def _():
        down_copy(d_out, d_in, d_sem.at[0], d_sem.at[1]).wait_recv()
        down_copy(n_out, n_in, n_sem.at[0], n_sem.at[1]).wait_recv()
        down_copy(rest_out, rest_in, n_sem.at[2], n_sem.at[3]).wait_recv()

    scale = 1.0 / (sum_d[0] + d_in[...].astype(F32) + floor_d)
    for plane in range(2):
        top = sum_n[plane, 0] - sum_d[0] * ext[plane, 0] + n_in[plane].astype(F32)
        rest = rest_in[plane].astype(F32)
        rest = jnp.concatenate(
            [rest[:, g * STEP : (g + 1) * STEP] for g in range(rows // STEP)], axis=0
        )
        top += jnp.concatenate([rest, jnp.zeros((width, rows - STEP), F32)], axis=1)
        x_new[plane] = obj[plane] + top * scale

    for block in range(n_chan):
        at = slice(block * share, (block + 1) * share)
        a_out[block, :used] = jnp.concatenate([x_new[0, at], x_new[1, at]], axis=0).astype(BF16)

    def chan_copy(src, dst, send, recv, step):
        other = (me + step) % n_chan
        return pltpu.make_async_remote_copy(
            src_ref=src.at[other],
            dst_ref=dst.at[me],
            send_sem=send.at[step - 1],
            recv_sem=recv.at[step - 1],
            device_id=chan_id(other),
            device_id_type=MESH,
        )

    for step in range(1, n_chan):
        chan_copy(a_out, a_in, a_send, a_recv, step).start()
    pd_all[t] = pd[...].astype(BF16)
    pn_all[t] = (pn[...] - probe_t[...] * pd[...]).astype(BF16)

    def probe_copy(buffer, send, recv, step):
        return pltpu.make_async_remote_copy(
            src_ref=buffer.at[t],
            dst_ref=buffer.at[t],
            send_sem=send.at[step - 1],
            recv_sem=recv.at[step - 1],
            device_id=tile_id((t + step) % n_tile),
            device_id_type=MESH,
        )

    for step in range(1, n_tile):
        probe_copy(pd_all, pd_send, pd_recv, step).start()
        probe_copy(pn_all, pn_send, pn_recv, step).start()
    a_in[me] = a_out[me]
    for i in range(5, 8):
        loads[i].wait()
    for step in range(1, n_chan):
        chan_copy(a_out, a_in, a_send, a_recv, step).wait_recv()

    spectra = [a_in[e].astype(F32) for e in range(n_chan)]
    shrunk = []
    for k in range(comps):
        c = analysis[k, 0] * spectra[0]
        for e in range(1, n_chan):
            c += analysis[k, e] * spectra[e]
        limit = thr[k]
        shrunk.append(c - jnp.minimum(jnp.maximum(c, -limit), limit))
    for e in range(n_chan):
        x = basis[e, 0] * shrunk[0]
        for k in range(1, comps):
            x += basis[e, k] * shrunk[k]
        b_out[e] = x.astype(BF16)

    for step in range(1, n_chan):
        chan_copy(b_out, b_in, b_send, b_recv, step).start()
    b_in[me] = b_out[me]

    for step in range(1, n_tile):
        probe_copy(pd_all, pd_send, pd_recv, step).wait_recv()
        probe_copy(pn_all, pn_send, pn_recv, step).wait_recv()
    den = pd_all[0].astype(F32)
    for other in range(1, n_tile):
        den += pd_all[other].astype(F32)
    scale = 1.0 / (den + 0.1 * jnp.max(den) + 1e-06)
    for c in range(2):
        for m in range(modes):
            num = pn_all[0, c, m].astype(F32)
            for other in range(1, n_tile):
                num += pn_all[other, c, m].astype(F32)
            out_probe[c, m] = probe[c, m] + (num * scale).T

    for step in range(1, n_chan):
        chan_copy(b_out, b_in, b_send, b_recv, step).wait_recv()
    for block in range(n_chan):
        at = slice(block * share, (block + 1) * share)
        back = b_in[block].astype(F32)
        out_obj[0, at] = 0.5 * x_new[0, at] + 0.5 * back[:share]
        out_obj[1, at] = 0.5 * x_new[1, at] + 0.5 * back[share:used]

    @pl.when(jnp.logical_not(first))
    def _():
        halo_copy(0).wait_send()
        halo_copy(1).wait_send()

    @pl.when(jnp.logical_not(last))
    def _():
        down_copy(d_out, d_in, d_sem.at[0], d_sem.at[1]).wait_send()
        down_copy(n_out, n_in, n_sem.at[0], n_sem.at[1]).wait_send()
        down_copy(rest_out, rest_in, n_sem.at[2], n_sem.at[3]).wait_send()

    for step in range(1, n_tile):
        probe_copy(pd_all, pd_send, pd_recv, step).wait_send()
        probe_copy(pn_all, pn_send, pn_recv, step).wait_send()
    for step in range(1, n_chan):
        chan_copy(a_out, a_in, a_send, a_recv, step).wait_send()
        chan_copy(b_out, b_in, b_send, b_recv, step).wait_send()


def body(sizes, object_field, probe_field, modulus, offsets, spectra_basis, analysis, threshold):
    n_energy, n_mode, n_tile = sizes
    n_chan = n_energy * n_mode
    extent = probe_field.shape[-1]
    modes = probe_field.shape[1]
    rows, width = object_field.shape[2:]
    share = -(-2 * (width // n_chan) // 16) * 16
    positions = offsets.shape[0]
    hbm = pl.BlockSpec(memory_space=pltpu.HBM)
    vmem = pl.BlockSpec(memory_space=pltpu.VMEM)
    dma = pltpu.SemaphoreType.DMA
    peers = max(1, n_tile - 1)
    flops = positions * modes * 4 * 2 * (2 * extent) ** 2 * extent
    dft = dft_parts(extent)
    out_obj, out_probe = pl.pallas_call(
        functools.partial(kernel, sizes),
        out_shape=(
            pltpu.VMEM((2, width, rows), F32),
            pltpu.VMEM((2, modes, extent, extent), F32),
        ),
        in_specs=[hbm] * 8,
        out_specs=(vmem, vmem),
        scratch_shapes=[
            pltpu.SMEM(offsets.shape[::-1], jnp.int32),
            pltpu.SMEM(spectra_basis.shape, F32),
            pltpu.SMEM(analysis.shape, F32),
            pltpu.SMEM(threshold.shape, F32),
            pltpu.VMEM(dft.shape, BF16),
            pltpu.VMEM((2, width, rows), F32),
            pltpu.VMEM((2, modes, extent, extent), F32),
            pltpu.VMEM((positions, extent, extent), BF16),
            dma((8,)),
            pltpu.VMEM((2 * extent, 2 * extent), BF16),
            pltpu.VMEM((2 * extent, 2 * extent), BF16),
            pltpu.VMEM((2, modes, extent, extent), F32),
            pltpu.VMEM((2, 2, width, rows), F32),
            pltpu.VMEM((extent, extent), F32),
            pltpu.VMEM((2 * PCOLS, 2, extent + 2 * STEP, rows), F32),
            pltpu.VMEM((2, 2, width, rows), F32),
            pltpu.VMEM((2, width, rows), F32),
            pltpu.VMEM((2, modes, extent, extent), F32),
            pltpu.VMEM((extent, extent), F32),
            pltpu.VMEM((2, 2, width // 2, rows), BF16),
            pltpu.VMEM((2, 2, width // 2, rows), BF16),
            pltpu.VMEM((width, rows), BF16),
            pltpu.VMEM((width, rows), BF16),
            pltpu.VMEM((2, width, rows), BF16),
            pltpu.VMEM((2, width, rows), BF16),
            pltpu.VMEM((2, width // (rows // STEP), rows), BF16),
            pltpu.VMEM((2, width // (rows // STEP), rows), BF16),
            pltpu.VMEM((n_tile, 2, modes, extent, extent), BF16),
            pltpu.VMEM((n_tile, extent, extent), BF16),
            pltpu.VMEM((2, width, rows), F32),
            pltpu.VMEM((n_chan, share, rows), BF16),
            pltpu.VMEM((n_chan, share, rows), BF16),
            pltpu.VMEM((n_chan, share, rows), BF16),
            pltpu.VMEM((n_chan, share, rows), BF16),
            dma((4,)),
            dma((2,)),
            dma((4,)),
            dma((peers,)),
            dma((peers,)),
            dma((peers,)),
            dma((peers,)),
            dma((n_chan - 1,)),
            dma((n_chan - 1,)),
            dma((n_chan - 1,)),
            dma((n_chan - 1,)),
        ],
        compiler_params=pltpu.CompilerParams(
            collective_id=0, has_side_effects=True, vmem_limit_bytes=58 * 1024 * 1024
        ),
        cost_estimate=pl.CostEstimate(flops=flops, bytes_accessed=2000000, transcendentals=0),
    )(
        offsets.T,
        spectra_basis,
        analysis,
        threshold,
        jnp.asarray(dft),
        jnp.swapaxes(object_field, 2, 3).reshape(2, width, rows),
        probe_field.reshape(2, modes, extent, extent),
        modulus.reshape(positions, extent, extent),
    )
    return (jnp.swapaxes(out_obj, 1, 2)[:, None], out_probe[:, :, None])


def solution(mesh):
    sizes = (mesh.shape["energy"], mesh.shape["mode"], mesh.shape["tile"])
    placed = (
        P(None, ("groups", "energy", "mode"), "tile", None),
        P(None, None, ("groups", "energy", "mode"), None, None),
        P(("groups", "energy", "mode"), "tile", None, None),
        P(("groups", "tile"), None),
        P(),
        P(),
        P(),
    )
    return jax.shard_map(
        functools.partial(body, sizes),
        mesh=mesh,
        in_specs=placed,
        out_specs=(
            P(None, ("groups", "energy", "mode"), "tile", None),
            P(None, None, ("groups", "energy", "mode"), None, None),
        ),
        check_vma=False,
    )
```

```python
import functools
import math

import jax
import jax.numpy as jnp
import numpy as np
from jax import lax
from jax.experimental import pallas as pl
from jax.experimental.pallas import tpu as pltpu
from jax.sharding import PartitionSpec as P

PCOLS = 2
STEP = 32
MESH = pl.DeviceIdType.MESH
BF16 = jnp.bfloat16
F32 = jnp.float32


def dft_parts(extent):
    counter = np.arange(extent)
    phases = -2.0 * math.pi / extent * (counter[:, None] * counter[None, :] % extent)
    norm = 1.0 / math.sqrt(extent)
    cosine = (np.cos(phases) * norm).astype(np.float32)
    sine = (np.sin(phases) * norm).astype(np.float32)
    return np.concatenate([cosine, sine], axis=1).astype(jnp.bfloat16)


def dot(left, right):
    return jnp.dot(left, right, preferred_element_type=F32)


def kernel(
    sizes,
    off_hbm,
    basis_hbm,
    analysis_hbm,
    thr_hbm,
    dft_hbm,
    obj_hbm,
    probe_hbm,
    mod_hbm,
    out_obj,
    out_probe,
    off,
    basis,
    analysis,
    thr,
    dft,
    obj,
    probe,
    mod,
    load_sem,
    fwd,
    bwd,
    probe_t,
    mod_t,
    ext,
    power,
    place,
    sum_n,
    sum_d,
    pn,
    pd,
    halo_out,
    halo_in,
    d_out,
    d_in,
    n_out,
    n_in,
    rest_out,
    rest_in,
    pn_all,
    pd_all,
    x_new,
    a_out,
    a_in,
    b_out,
    b_in,
    halo_sem,
    d_sem,
    n_sem,
    pn_send,
    pn_recv,
    pd_send,
    pd_recv,
    a_send,
    a_recv,
    b_send,
    b_recv,
):
    n_energy, n_mode, n_tile = sizes
    n_chan = n_energy * n_mode
    t = lax.axis_index("tile")
    me = lax.axis_index("energy") * n_mode + lax.axis_index("mode")
    modes, extent = probe.shape[1], probe.shape[2]
    width, rows = obj.shape[1], obj.shape[2]
    positions = mod.shape[0]
    share = width // n_chan
    used = 2 * share
    comps = thr.shape[0]

    def tile_id(other):
        return {"tile": other}

    def chan_id(other):
        return {"energy": other // n_mode, "mode": other % n_mode}

    barrier = pltpu.get_barrier_semaphore()
    for step in range(1, n_chan):
        pl.semaphore_signal(
            barrier, inc=1, device_id=chan_id((me + step) % n_chan), device_id_type=MESH
        )
    for step in range(1, n_tile):
        pl.semaphore_signal(
            barrier, inc=1, device_id=tile_id((t + step) % n_tile), device_id_type=MESH
        )

    pairs = [
        (obj_hbm, obj),
        (off_hbm, off),
        (probe_hbm, probe),
        (dft_hbm, dft),
        (mod_hbm, mod),
        (analysis_hbm, analysis),
        (basis_hbm, basis),
        (thr_hbm, thr),
    ]
    loads = [
        pltpu.make_async_copy(src, dst, load_sem.at[i]) for i, (src, dst) in enumerate(pairs)
    ]
    for load in loads:
        load.start()

    place[...] = jnp.zeros_like(place)
    sum_n[...] = jnp.zeros_like(sum_n)
    sum_d[...] = jnp.zeros_like(sum_d)
    pn[...] = jnp.zeros_like(pn)
    pd[...] = jnp.zeros_like(pd)

    loads[0].wait()
    near, fold = width // 2, rows // 2
    for part in range(2):
        halo_out[part] = jnp.concatenate(
            [
                obj[:, :near, part * fold : (part + 1) * fold],
                obj[:, near:, part * fold : (part + 1) * fold],
            ],
            axis=2,
        ).astype(BF16)
    ext[:, 0] = obj[...].astype(BF16).astype(F32)

    pl.semaphore_wait(barrier, n_chan - 1 + n_tile - 1)

    def halo_copy(part):
        return pltpu.make_async_remote_copy(
            src_ref=halo_out.at[part],
            dst_ref=halo_in.at[part],
            send_sem=halo_sem.at[part],
            recv_sem=halo_sem.at[2 + part],
            device_id=tile_id((t + n_tile - 1) % n_tile),
            device_id_type=MESH,
        )

    def down_copy(src, dst, send, recv):
        return pltpu.make_async_remote_copy(
            src_ref=src,
            dst_ref=dst,
            send_sem=send,
            recv_sem=recv,
            device_id=tile_id((t + 1) % n_tile),
            device_id_type=MESH,
        )

    first = t == 0
    last = t == n_tile - 1

    @pl.when(jnp.logical_not(first))
    def _():
        halo_copy(0).start()
        halo_copy(1).start()

    loads[2].wait()
    total = jnp.zeros((extent, extent), F32)
    for m in range(modes):
        for c in range(2):
            turned = probe[c, m].T
            probe_t[c, m] = turned
            total += turned * turned
    power[...] = total
    floor_d = 0.1 * jnp.max(total) + 1e-06
    span = extent + STEP
    lane = lax.broadcasted_iota(jnp.int32, (extent, rows), 1)

    def lay(plane, block, row):
        moved = pltpu.roll(block, row, axis=1)
        inside = lane >= row
        place[plane, 0, STEP : STEP + extent] = jnp.where(inside, moved, 0.0)
        place[plane, 1, STEP : STEP + extent] = jnp.where(inside, 0.0, moved)

    loads[1].wait()

    def put_power(k, carry):
        for c in range(PCOLS):
            q = k * PCOLS + c
            lay(c, power[...], STEP * k + off[0, q])
            for b in range(2):
                sum_d[b, STEP * c : STEP * c + span] += place[
                    c, b, pl.ds(STEP - off[1, q], span)
                ]
        return carry

    lax.fori_loop(0, positions // PCOLS, put_power, 0)

    d_out[...] = sum_d[1].astype(BF16)

    loads[3].wait()
    cosine = dft[:, :extent]
    sine = dft[:, extent:]
    fwd[:extent, :extent] = cosine
    fwd[extent:, extent:] = cosine
    fwd[:extent, extent:] = -sine
    fwd[extent:, :extent] = sine
    bwd[:extent, :extent] = cosine
    bwd[extent:, extent:] = cosine
    bwd[:extent, extent:] = sine
    bwd[extent:, :extent] = -sine
    loads[4].wait()

    def turn(q, carry):
        mod_t[q] = mod[q].astype(F32).T
        return carry

    lax.fori_loop(0, positions, turn, 0)

    def take_halo(part):
        halo_copy(part).wait_recv()
        packed = halo_in[part].astype(F32)
        ext[:, 1, :near, part * fold : (part + 1) * fold] = packed[:, :, :fold]
        ext[:, 1, near:, part * fold : (part + 1) * fold] = packed[:, :, fold:]

    @pl.when(jnp.logical_not(last))
    def _():
        down_copy(d_out, d_in, d_sem.at[0], d_sem.at[1]).start()
        take_halo(0)

    @pl.when(last)
    def _():
        ext[:, 1] = jnp.zeros((2, width, rows), F32)

    def window(plane, row, col):
        back = lax.rem(rows - row, rows)
        here, below = (
            pltpu.roll(ext[plane, b, pl.ds(col, extent)], back, axis=1) for b in range(2)
        )
        return jnp.where(lane < rows - row, here, below)

    def lanes_of(array, index):
        return array[:, index * extent : (index + 1) * extent]

    def rows_of(array, index):
        return array[index * extent : (index + 1) * extent]

    turns = positions // PCOLS
    group = width // (rows // STEP)

    def send_most():
        for plane in range(2):
            n_out[plane] = (sum_n[plane, 1] - sum_d[1] * ext[plane, 1]).astype(BF16)
            sum_n[plane, 1] = jnp.zeros((width, rows), F32)

        @pl.when(jnp.logical_not(last))
        def _():
            down_copy(n_out, n_in, n_sem.at[0], n_sem.at[1]).start()

    def one(i, carry):
        k = (i + 1) % turns

        if i == min(1, turns - 1):

            @pl.when(jnp.logical_not(last))
            def _():
                take_halo(1)

        if i == turns - 1:
            send_most()

        objects, tall = [], []
        for c in range(PCOLS):
            q = k * PCOLS + c
            row, col = STEP * k + off[0, q], STEP * c + off[1, q]
            o_r, o_i = window(0, row, col), window(1, row, col)
            objects.append((o_r, o_i))
            for m in range(modes):
                p_r, p_i = probe_t[0, m], probe_t[1, m]
                tall.append(
                    jnp.concatenate(
                        [p_r * o_r - p_i * o_i, p_r * o_i + p_i * o_r], axis=1
                    ).astype(BF16)
                )
        n_c = []
        waves = range(PCOLS * modes)
        half = dot(jnp.concatenate(tall, axis=0), bwd[...])
        wide = jnp.concatenate(
            [
                jnp.concatenate(
                    [rows_of(half, w)[:, :extent], rows_of(half, w)[:, extent:]], axis=0
                )
                for w in waves
            ],
            axis=1,
        ).astype(BF16)
        spec = dot(fwd[...], wide)
        scaled = []
        for c in range(PCOLS):
            parts = [lanes_of(spec, c * modes + m) for m in range(modes)]
            squares = parts[0] * parts[0]
            for m in range(1, modes):
                squares += parts[m] * parts[m]
            mag = squares[:extent] + squares[extent:]
            factor = mod_t[k * PCOLS + c] * lax.rsqrt(mag + 0.01)
            both = jnp.concatenate([factor, factor], axis=0)
            scaled += [(part * both).astype(BF16) for part in parts]
        ret = dot(bwd[...], jnp.concatenate(scaled, axis=1))
        cols = jnp.concatenate(
            [
                jnp.concatenate(
                    [lanes_of(ret, w)[:extent], lanes_of(ret, w)[extent:]], axis=1
                )
                for w in waves
            ],
            axis=0,
        ).astype(BF16)
        wave = dot(cols, fwd[...])
        for c in range(PCOLS):
            n_r = jnp.zeros((extent, extent), F32)
            n_i = jnp.zeros((extent, extent), F32)
            for m in range(modes):
                p_r, p_i = probe_t[0, m], probe_t[1, m]
                got = rows_of(wave, c * modes + m)
                w_r, w_i = got[:, :extent], got[:, extent:]
                n_r += p_r * w_r + p_i * w_i
                n_i += p_r * w_i - p_i * w_r
            n_c.append((n_r, n_i))
        for m in range(modes):
            pn_r, pn_i = pn[0, m], pn[1, m]
            for c in range(PCOLS):
                o_r, o_i = objects[c]
                got = rows_of(wave, c * modes + m)
                w_r, w_i = got[:, :extent], got[:, extent:]
                pn_r += o_r * w_r + o_i * w_i
                pn_i += o_r * w_i - o_i * w_r
            pn[0, m] = pn_r
            pn[1, m] = pn_i
        weight = pd[...]
        for o_r, o_i in objects:
            weight += o_r * o_r + o_i * o_i
        pd[...] = weight
        for c in range(PCOLS):
            q = k * PCOLS + c
            for plane in range(2):
                lay(2 * c + plane, n_c[c][plane], STEP * k + off[0, q])
        for c in range(PCOLS):
            q = k * PCOLS + c
            for plane in range(2):
                for b in range(2):
                    sum_n[plane, b, STEP * c : STEP * c + span] += place[
                        2 * c + plane, b, pl.ds(STEP - off[1, q], span)
                    ]
        return carry

    for i in range(turns):
        one(i, 0)

    for plane in range(2):
        rest_out[plane] = jnp.concatenate(
            [
                sum_n[plane, 1, g * group : (g + 1) * group, :STEP]
                for g in range(rows // STEP)
            ],
            axis=1,
        ).astype(BF16)

    @pl.when(jnp.logical_not(last))
    def _():
        down_copy(rest_out, rest_in, n_sem.at[2], n_sem.at[3]).start()

    @pl.when(first)
    def _():
        n_in[...] = jnp.zeros_like(n_in)
        rest_in[...] = jnp.zeros_like(rest_in)
        d_in[...] = jnp.zeros_like(d_in)

    @pl.when(jnp.logical_not(first))
    def _():
        down_copy(d_out, d_in, d_sem.at[0], d_sem.at[1]).wait_recv()
        down_copy(n_out, n_in, n_sem.at[0], n_sem.at[1]).wait_recv()
        down_copy(rest_out, rest_in, n_sem.at[2], n_sem.at[3]).wait_recv()

    scale = 1.0 / (sum_d[0] + d_in[...].astype(F32) + floor_d)
    for plane in range(2):
        top = sum_n[plane, 0] - sum_d[0] * ext[plane, 0] + n_in[plane].astype(F32)
        rest = rest_in[plane].astype(F32)
        rest = jnp.concatenate(
            [rest[:, g * STEP : (g + 1) * STEP] for g in range(rows // STEP)], axis=0
        )
        top += jnp.concatenate([rest, jnp.zeros((width, rows - STEP), F32)], axis=1)
        x_new[plane] = obj[plane] + top * scale

    for block in range(n_chan):
        at = slice(block * share, (block + 1) * share)
        a_out[block, :used] = jnp.concatenate([x_new[0, at], x_new[1, at]], axis=0).astype(BF16)

    def peer(step):
        other, bit = me, 1
        while bit < n_chan:
            if step & bit:
                other = other + bit - 2 * bit * ((me // bit) % 2)
            bit *= 2
        return other

    def chan_copy(src, dst, send, recv, step):
        other = peer(step)
        return pltpu.make_async_remote_copy(
            src_ref=src.at[other],
            dst_ref=dst.at[me],
            send_sem=send.at[step - 1],
            recv_sem=recv.at[step - 1],
            device_id=chan_id(other),
            device_id_type=MESH,
        )

    for step in range(n_chan - 1, 0, -1):
        chan_copy(a_out, a_in, a_send, a_recv, step).start()
    pd_all[t] = pd[...].astype(BF16)
    pn_all[t] = (pn[...] - probe_t[...] * pd[...]).astype(BF16)

    def probe_copy(buffer, send, recv, step):
        return pltpu.make_async_remote_copy(
            src_ref=buffer.at[t],
            dst_ref=buffer.at[t],
            send_sem=send.at[step - 1],
            recv_sem=recv.at[step - 1],
            device_id=tile_id((t + step) % n_tile),
            device_id_type=MESH,
        )

    for step in range(1, n_tile):
        probe_copy(pd_all, pd_send, pd_recv, step).start()
        probe_copy(pn_all, pn_send, pn_recv, step).start()
    for i in range(5, 8):
        loads[i].wait()
    spectrum = a_out[me].astype(F32)
    total = [analysis[k, me] * spectrum for k in range(comps)]
    for step in range(1, n_chan):
        chan_copy(a_out, a_in, a_send, a_recv, step).wait_recv()
        spectrum = a_in[peer(step)].astype(F32)
        total = [total[k] + analysis[k, peer(step)] * spectrum for k in range(comps)]
    shrunk = [
        total[k] - jnp.minimum(jnp.maximum(total[k], -thr[k]), thr[k]) for k in range(comps)
    ]

    def project(e):
        x = basis[e, 0] * shrunk[0]
        for k in range(1, comps):
            x += basis[e, k] * shrunk[k]
        return x.astype(BF16)

    for step in range(n_chan - 1, 0, -1):
        b_out[peer(step)] = project(peer(step))
        chan_copy(b_out, b_in, b_send, b_recv, step).start()
    b_in[me] = project(me)

    for step in range(1, n_tile):
        probe_copy(pd_all, pd_send, pd_recv, step).wait_recv()
        probe_copy(pn_all, pn_send, pn_recv, step).wait_recv()
    den = pd_all[0].astype(F32)
    for other in range(1, n_tile):
        den += pd_all[other].astype(F32)
    scale = 1.0 / (den + 0.1 * jnp.max(den) + 1e-06)
    for c in range(2):
        for m in range(modes):
            num = pn_all[0, c, m].astype(F32)
            for other in range(1, n_tile):
                num += pn_all[other, c, m].astype(F32)
            out_probe[c, m] = probe[c, m] + (num * scale).T

    for step in range(1, n_chan):
        chan_copy(b_out, b_in, b_send, b_recv, step).wait_recv()
    for block in range(n_chan):
        at = slice(block * share, (block + 1) * share)
        back = b_in[block].astype(F32)
        out_obj[0, at] = 0.5 * x_new[0, at] + 0.5 * back[:share]
        out_obj[1, at] = 0.5 * x_new[1, at] + 0.5 * back[share:used]

    @pl.when(jnp.logical_not(first))
    def _():
        halo_copy(0).wait_send()
        halo_copy(1).wait_send()

    @pl.when(jnp.logical_not(last))
    def _():
        down_copy(d_out, d_in, d_sem.at[0], d_sem.at[1]).wait_send()
        down_copy(n_out, n_in, n_sem.at[0], n_sem.at[1]).wait_send()
        down_copy(rest_out, rest_in, n_sem.at[2], n_sem.at[3]).wait_send()

    for step in range(1, n_tile):
        probe_copy(pd_all, pd_send, pd_recv, step).wait_send()
        probe_copy(pn_all, pn_send, pn_recv, step).wait_send()
    for step in range(1, n_chan):
        chan_copy(a_out, a_in, a_send, a_recv, step).wait_send()
        chan_copy(b_out, b_in, b_send, b_recv, step).wait_send()


def body(sizes, object_field, probe_field, modulus, offsets, spectra_basis, analysis, threshold):
    n_energy, n_mode, n_tile = sizes
    n_chan = n_energy * n_mode
    extent = probe_field.shape[-1]
    modes = probe_field.shape[1]
    rows, width = object_field.shape[2:]
    share = -(-2 * (width // n_chan) // 16) * 16
    positions = offsets.shape[0]
    hbm = pl.BlockSpec(memory_space=pltpu.HBM)
    vmem = pl.BlockSpec(memory_space=pltpu.VMEM)
    dma = pltpu.SemaphoreType.DMA
    peers = max(1, n_tile - 1)
    flops = positions * modes * 4 * 2 * (2 * extent) ** 2 * extent
    dft = dft_parts(extent)
    out_obj, out_probe = pl.pallas_call(
        functools.partial(kernel, sizes),
        out_shape=(
            pltpu.VMEM((2, width, rows), F32),
            pltpu.VMEM((2, modes, extent, extent), F32),
        ),
        in_specs=[hbm] * 8,
        out_specs=(vmem, vmem),
        scratch_shapes=[
            pltpu.SMEM(offsets.shape[::-1], jnp.int32),
            pltpu.SMEM(spectra_basis.shape, F32),
            pltpu.SMEM(analysis.shape, F32),
            pltpu.SMEM(threshold.shape, F32),
            pltpu.VMEM(dft.shape, BF16),
            pltpu.VMEM((2, width, rows), F32),
            pltpu.VMEM((2, modes, extent, extent), F32),
            pltpu.VMEM((positions, extent, extent), BF16),
            dma((8,)),
            pltpu.VMEM((2 * extent, 2 * extent), BF16),
            pltpu.VMEM((2 * extent, 2 * extent), BF16),
            pltpu.VMEM((2, modes, extent, extent), F32),
            pltpu.VMEM((positions, extent, extent), F32),
            pltpu.VMEM((2, 2, width, rows), F32),
            pltpu.VMEM((extent, extent), F32),
            pltpu.VMEM((2 * PCOLS, 2, extent + 2 * STEP, rows), F32),
            pltpu.VMEM((2, 2, width, rows), F32),
            pltpu.VMEM((2, width, rows), F32),
            pltpu.VMEM((2, modes, extent, extent), F32),
            pltpu.VMEM((extent, extent), F32),
            pltpu.VMEM((2, 2, width // 2, rows), BF16),
            pltpu.VMEM((2, 2, width // 2, rows), BF16),
            pltpu.VMEM((width, rows), BF16),
            pltpu.VMEM((width, rows), BF16),
            pltpu.VMEM((2, width, rows), BF16),
            pltpu.VMEM((2, width, rows), BF16),
            pltpu.VMEM((2, width // (rows // STEP), rows), BF16),
            pltpu.VMEM((2, width // (rows // STEP), rows), BF16),
            pltpu.VMEM((n_tile, 2, modes, extent, extent), BF16),
            pltpu.VMEM((n_tile, extent, extent), BF16),
            pltpu.VMEM((2, width, rows), F32),
            pltpu.VMEM((n_chan, share, rows), BF16),
            pltpu.VMEM((n_chan, share, rows), BF16),
            pltpu.VMEM((n_chan, share, rows), BF16),
            pltpu.VMEM((n_chan, share, rows), BF16),
            dma((4,)),
            dma((2,)),
            dma((4,)),
            dma((peers,)),
            dma((peers,)),
            dma((peers,)),
            dma((peers,)),
            dma((n_chan - 1,)),
            dma((n_chan - 1,)),
            dma((n_chan - 1,)),
            dma((n_chan - 1,)),
        ],
        compiler_params=pltpu.CompilerParams(
            collective_id=0, has_side_effects=True, vmem_limit_bytes=58 * 1024 * 1024
        ),
        cost_estimate=pl.CostEstimate(flops=flops, bytes_accessed=2000000, transcendentals=0),
    )(
        offsets.T,
        spectra_basis,
        analysis,
        threshold,
        jnp.asarray(dft),
        jnp.swapaxes(object_field, 2, 3).reshape(2, width, rows),
        probe_field.reshape(2, modes, extent, extent),
        modulus.reshape(positions, extent, extent),
    )
    return (jnp.swapaxes(out_obj, 1, 2)[:, None], out_probe[:, :, None])


def solution(mesh):
    sizes = (mesh.shape["energy"], mesh.shape["mode"], mesh.shape["tile"])
    placed = (
        P(None, ("groups", "energy", "mode"), "tile", None),
        P(None, None, ("groups", "energy", "mode"), None, None),
        P(("groups", "energy", "mode"), "tile", None, None),
        P(("groups", "tile"), None),
        P(),
        P(),
        P(),
    )
    return jax.shard_map(
        functools.partial(body, sizes),
        mesh=mesh,
        in_specs=placed,
        out_specs=(
            P(None, ("groups", "energy", "mode"), "tile", None),
            P(None, None, ("groups", "energy", "mode"), None, None),
        ),
        check_vma=False,
    )
```
